32 devices in a mesh: tunnel: 8 (over y, x, core), width: 4 (over z).
Axes of the slice: x: 2, y: 2, z: 4, core: 2. Of those that a mesh axis runs over, the one named last changes fastest.
Arguments:
- source: float32 [512, 128, 512], P('tunnel', 'width'), may hold values from -6 to 6
- initial: float32 [512, 128, 512], P('tunnel', 'width'), may hold values from -6 to 6
- diffusivity: float32 [512, 128, 512], P('tunnel', 'width'), may hold values from 0.5 to 2
- reaction: float32 [512, 128, 512], P('tunnel', 'width'), may hold values from 0.05 to 0.5
Outputs:
- smoothed: float32 [512, 128, 512], P('tunnel', 'width')
- coarse_residual: float32 [256, 64, 256], P('tunnel')
The draws below stay inside these ranges and needn't reach their ends.
All inputs are finite; a program needn't handle non-finite values.
Results may differ from the reference program's by a relative error of at most 0.00013.
Values sent between devices are 32-bit elements; how exact they have to be, the bound alone decides.
A program may use at most 192 MiB of HBM per device.

```python
import math
import jax
import jax.numpy as jnp
from jax import lax

NZ = 512
PASSES = 4
NX = 512
NY = 128


def shard_levels(key, extent, split, low, top_value):
    def one(dim, parts):
        heights = jax.random.uniform(jax.random.fold_in(jax.random.fold_in(key, 6), dim), (parts,), jnp.float32, low / len(split), top_value / len(split))
        return jnp.repeat(jnp.exp(heights), extent[dim] // parts).reshape((-1,) + (1,) * (len(extent) - dim - 1))

    factor_of = one(*split[0])
    for cut in split[1:]:
        factor_of = factor_of * one(*cut)
    return factor_of


def centred(rng, dims, spread, bound, shards=(), dtype=jnp.bfloat16):
    gain = shard_levels(rng, dims, shards, -0.22, 0.18) if shards else 1.0
    drawn = jax.random.normal(rng, dims, jnp.float32) * spread * gain
    return jnp.minimum(jnp.maximum(drawn, -bound), bound).astype(dtype)


def setup_inputs(seed: int = 0) -> dict:
    splits = jax.random.split(jax.random.key(seed), 5)
    return {
        "source": centred(splits[0], (NX, NY, NZ), 1.0, 6.0, ((0, 8), (1, 4)), jnp.float32),
        "initial": centred(splits[1], (NX, NY, NZ), 1.0, 6.0, ((0, 8), (1, 4)), jnp.float32),
        "diffusivity": jnp.clip(jnp.exp(math.log(2.0) - 1.3862944 * jax.random.uniform(splits[2], (NX, NY, NZ), jnp.float32) ** shard_levels(splits[2], (NX, NY, NZ), ((0, 8), (1, 4)), -0.2, 0.2)), 0.5, 2.0),
        "reaction": jnp.clip(jnp.exp(math.log(0.5) - 2.3025851 * jax.random.uniform(splits[3], (NX, NY, NZ), jnp.float32) ** shard_levels(splits[3], (NX, NY, NZ), ((0, 8), (1, 4)), -0.2, 0.2)), 0.05, 0.5),
    }


relax_weight = 0.8
settle_rate = 0.5


def operate(field, diffusivity, reaction):
    padded = jnp.pad(field, 1)
    centre = padded[1:-1, 1:-1, 1:-1]
    beside_x = padded[2:, 1:-1, 1:-1] + padded[:-2, 1:-1, 1:-1]
    beside_y = padded[1:-1, 2:, 1:-1] + padded[1:-1, :-2, 1:-1]
    upper_cell = padded[1:-1, 1:-1, 2:]
    beside_z = upper_cell + padded[1:-1, 1:-1, :-2]
    diagonal = reaction + 11.0 * diffusivity + settle_rate
    image = diagonal * centre - diffusivity * (2.5 * (beside_x + beside_y) + 0.5 * beside_z) - settle_rate * upper_cell
    return image, diagonal


def restrict_axis(values, along):
    count = values.shape[along]
    widths = [(0, 0), (0, 0), (0, 0)]
    widths[along] = (1, 0)
    padded = jnp.pad(values, widths)
    first = lax.slice_in_dim(padded, 0, count, 2, along)
    middle = lax.slice_in_dim(padded, 1, count + 1, 2, along)
    last = lax.slice_in_dim(padded, 2, count + 1, 2, along)
    return 0.25 * first + 0.5 * middle + 0.25 * last


def reference(source, initial, diffusivity, reaction):
    field = initial
    for sweep in range(PASSES):
        image, diagonal = operate(field, diffusivity, reaction)
        field = field + relax_weight * (source - image) / diagonal
    image, diagonal = operate(field, diffusivity, reaction)
    residual = source - image
    coarse = restrict_axis(restrict_axis(restrict_axis(residual, 0), 1), 2)
    return field, coarse
```

```python
import functools

import jax
import jax.numpy as jnp
from jax import lax
from jax.experimental import pallas as pl
from jax.experimental.pallas import tpu as pltpu
from jax.sharding import PartitionSpec as P

PASSES = 4
CHUNKS = 4
EDGE = CHUNKS
TOP = 8

relax_weight = 0.8
settle_rate = 0.5
MESH = pl.DeviceIdType.MESH


def kernel(
    n_tunnel,
    n_width,
    source,
    initial,
    diffusivity,
    reaction,
    smoothed,
    coarse,
    va,
    vb,
    src,
    dif,
    rea,
    rec,
    ys,
    yr,
    resid,
    table,
    q,
    yb,
    ycs,
    ycr,
    cz,
    x_send,
    x_recv,
    y_send,
    y_recv,
    q_sem,
    c_send,
    c_recv,
    g_send,
    g_recv,
    in_sem,
    v_sem,
    out_sem,
    own_sem,
):
    planes, rows, height = source.shape
    span = planes // CHUNKS
    tiles = rows // 8
    half = rows // 2
    low = height // 2
    per = span // 2
    t_me = lax.axis_index("tunnel")
    w_me = lax.axis_index("width")
    t_has = (t_me > 0, t_me < n_tunnel - 1)
    w_has = (w_me > 0, w_me < n_width - 1)
    t_to = (
        (jnp.maximum(t_me - 1, 0), w_me),
        (jnp.minimum(t_me + 1, n_tunnel - 1), w_me),
    )
    w_to = (
        (t_me, jnp.maximum(w_me - 1, 0)),
        (t_me, jnp.minimum(w_me + 1, n_width - 1)),
    )
    bufs = (va, vb)
    cells = pl.ds(TOP, rows)

    def bounds(c):
        first = max(span * c - 1, 0)
        last = planes if c == CHUNKS - 1 else span * c + span - 1
        return first, last - first

    load_v = pltpu.make_async_copy(initial, va.at[pl.ds(1, planes), cells, :], v_sem)
    load_v.start()
    loads = {}
    for c in (CHUNKS - 1, 0) + tuple(range(CHUNKS - 2, 0, -1)):
        first, count = bounds(c)
        for a, (hbm, mem) in enumerate(((source, src), (diffusivity, dif), (reaction, rea))):
            loads[a, c] = pltpu.make_async_copy(
                hbm.at[pl.ds(first, count)], mem.at[pl.ds(first, count)], in_sem.at[a, c]
            )
            loads[a, c].start()

    barrier = pltpu.get_barrier_semaphore()
    for d in range(2):

        @pl.when(t_has[d])
        def _():
            pl.semaphore_signal(barrier, inc=1, device_id=t_to[d], device_id_type=MESH)

    for d in range(1, n_width):
        peer = lax.rem(w_me + d, n_width)
        pl.semaphore_signal(barrier, inc=1, device_id=(t_me, peer), device_id_type=MESH)

    for d in range(2):

        @pl.when(jnp.logical_not(t_has[d]))
        def _():
            side = 0 if d == 0 else planes + 1
            for buf in bufs:
                buf[side, cells, :] = jnp.zeros((rows, height), jnp.float32)
            if d == 0:
                q[0] = jnp.zeros((rows, low), jnp.float32)

        @pl.when(jnp.logical_not(w_has[d]))
        def _():
            for k in range(PASSES + 1):
                yr[k, d] = jnp.zeros(yr.shape[2:], jnp.float32)
            if d == 0:
                ycr[...] = jnp.zeros(ycr.shape, jnp.float32)

    fine = lax.broadcasted_iota(jnp.int32, (height, low), 0)
    gap = fine - 2 * lax.broadcasted_iota(jnp.int32, (height, low), 1)
    weight = jnp.where(gap == 0, 0.5, jnp.where((gap == 1) | (gap == -1), 0.25, 0.0))
    table[...] = weight.astype(jnp.float32).astype(jnp.bfloat16)

    beside = jnp.where(t_has[0], 1, 0) + jnp.where(t_has[1], 1, 0)
    pl.semaphore_wait(barrier, n_width - 1 + beside)

    def x_copy(k, d):
        buf = bufs[k % 2]
        mine, theirs = (1, planes + 1) if d == 0 else (planes, 0)
        return pltpu.make_async_remote_copy(
            src_ref=buf.at[mine, cells, :],
            dst_ref=buf.at[theirs, cells, :],
            send_sem=x_send.at[k, d],
            recv_sem=x_recv.at[k, 1 - d],
            device_id=t_to[d],
            device_id_type=MESH,
        )

    def y_copy(k, d, c):
        if k == 0:
            part = pl.ds(0, ys.shape[2])
        elif c == EDGE:
            part = pl.ds(planes, 8)
        else:
            part = pl.ds(span * c, span)
        return pltpu.make_async_remote_copy(
            src_ref=ys.at[k, d, part, :],
            dst_ref=yr.at[k, 1 - d, part, :],
            send_sem=y_send.at[k, d, c],
            recv_sem=y_recv.at[k, 1 - d, c],
            device_id=w_to[d],
            device_id_type=MESH,
        )

    def start_x(k):
        for d in range(2):

            @pl.when(t_has[d])
            def _():
                x_copy(k, d).start()

    def sent_x(k):
        for d in range(2):

            @pl.when(t_has[d])
            def _():
                x_copy(k, d).wait_send()

    def got_x(k):
        for d in range(2):

            @pl.when(t_has[d])
            def _():
                x_copy(k, 1 - d).wait_recv()

    def start_y(k, c):
        for d in range(2):

            @pl.when(w_has[d])
            def _():
                y_copy(k, d, c).start()

    def sent_y(k, c):
        for d in range(2):

            @pl.when(w_has[d])
            def _():
                y_copy(k, d, c).wait_send()

    def got_y(k, c):
        for d in range(2):

            @pl.when(w_has[d])
            def _():
                y_copy(k, 1 - d, c).wait_recv()

    lane = lax.broadcasted_iota(jnp.int32, (8, 128), 1)

    def neighbours(v, p, t):
        here = pl.ds(TOP + 8 * t, 8)
        centre = v[p, here, :]
        beside = (
            v[p - 1, here, :]
            + v[p + 1, here, :]
            + (v[p, pl.ds(TOP + 8 * t - 1, 8), :] + v[p, pl.ds(TOP + 8 * t + 1, 8), :])
        )
        upper = pltpu.roll(centre, height - 1, 1)
        lower = pltpu.roll(centre, 1, 1)
        cut = height - 128
        upper = jnp.concatenate(
            [upper[:, :cut], jnp.where(lane == 127, 0.0, upper[:, cut:])], axis=1
        )
        lower = jnp.concatenate(
            [jnp.where(lane == 0, 0.0, lower[:, :128]), lower[:, 128:]], axis=1
        )
        return centre, 2.5 * beside + 0.5 * (upper + lower), upper

    def put_halo(k, p, row):
        v = bufs[k % 2]
        v[p, TOP - 1 : TOP, :] = yr[k, 0, pl.ds(row, 1), :]
        v[p, TOP + rows : TOP + rows + 1, :] = yr[k, 1, pl.ds(row, 1), :]

    def smooth_plane(k, p, row):
        v, new = bufs[(k - 1) % 2], bufs[k % 2]
        put_halo(k - 1, p, row)
        for t in range(tiles):
            at = pl.ds(8 * t, 8)
            centre, beside, upper = neighbours(v, p, t)
            spread = dif[p - 1, at, :]
            if k == 1:
                factor = relax_weight / (rea[p - 1, at, :] + 11.0 * spread + settle_rate)
                rec[p - 1, at, :] = factor
            else:
                factor = rec[p - 1, at, :]
            off = src[p - 1, at, :] + spread * beside + settle_rate * upper
            out = (1.0 - relax_weight) * centre + factor * off
            new[p, pl.ds(TOP + 8 * t, 8), :] = out
            if t == 0:
                ys[k, 0, pl.ds(row, 1), :] = out[0:1, :]
            if t == tiles - 1:
                ys[k, 1, pl.ds(row, 1), :] = out[7:8, :]

    def residual_plane(p, row, slot):
        v = bufs[PASSES % 2]
        put_halo(PASSES, p, row)
        for t in range(tiles):
            at = pl.ds(8 * t, 8)
            centre, beside, upper = neighbours(v, p, t)
            spread = dif[p - 1, at, :]
            diagonal = rea[p - 1, at, :] + 11.0 * spread + settle_rate
            resid[slot, at, :] = (
                src[p - 1, at, :]
                - diagonal * centre
                + spread * beside
                + settle_rate * upper
            )

    def restrict_height(count):
        r = resid[0:count].reshape(count * rows, height)
        hi = r.astype(jnp.bfloat16)
        lo = (r - hi.astype(jnp.float32)).astype(jnp.bfloat16)
        t = table[...]
        out = jnp.dot(hi, t, preferred_element_type=jnp.float32) + jnp.dot(
            lo, t, preferred_element_type=jnp.float32
        )
        return out.reshape(count, rows, low)

    load_v.wait()
    start_x(0)

    @pl.loop(1, planes + 1)
    def _(p):
        ys[0, 0, pl.ds(p, 1), :] = va[p, TOP : TOP + 1, :]
        ys[0, 1, pl.ds(p, 1), :] = va[p, TOP + rows - 1 : TOP + rows, :]

    ys[0, 0, planes + 1 : planes + 2, :] = va[1, TOP : TOP + 1, :]
    ys[0, 1, planes + 1 : planes + 2, :] = va[1, TOP + rows - 1 : TOP + rows, :]
    start_y(0, EDGE)

    order = tuple(range(CHUNKS - 1, -1, -1))
    stores = {}
    for k in range(1, PASSES + 1):
        if k >= 2:
            sent_x(k - 2)
        if k == 1:
            for c in (CHUNKS - 1, 0):
                for a in range(3):
                    loads[a, c].wait()
        got_x(k - 1)
        got_y(k - 1, EDGE)
        smooth_plane(k, planes, planes)
        smooth_plane(k, 1, planes + 1)
        start_x(k)
        start_y(k, EDGE)
        for c in order:
            if k == 1:
                if 0 < c < CHUNKS - 1:
                    for a in range(3):
                        loads[a, c].wait()
            else:
                got_y(k - 1, c)

            @pl.loop(max(span * c, 2), span * c + span)
            def _(p):
                smooth_plane(k, p, p)

            start_y(k, c)
            if k == PASSES:
                first, count = bounds(c)
                stores[c] = pltpu.make_async_copy(
                    bufs[k % 2].at[pl.ds(first + 1, count), cells, :],
                    smoothed.at[pl.ds(first, count)],
                    out_sem.at[c],
                )
                stores[c].start()

    def q_copy():
        return pltpu.make_async_remote_copy(
            src_ref=q.at[planes],
            dst_ref=q.at[0],
            send_sem=q_sem.at[0],
            recv_sem=q_sem.at[1],
            device_id=t_to[1],
            device_id_type=MESH,
        )

    def c_copy(c):
        part = pl.ds(per * c, per)
        return pltpu.make_async_remote_copy(
            src_ref=ycs.at[part, :],
            dst_ref=ycr.at[part, :],
            send_sem=c_send.at[c],
            recv_sem=c_recv.at[c],
            device_id=w_to[1],
            device_id_type=MESH,
        )

    def g_copy(c, owner, peer, d):
        part = pl.ds(per * c, per)
        return pltpu.make_async_remote_copy(
            src_ref=cz.at[part],
            dst_ref=coarse.at[part, pl.ds(pl.multiple_of(owner * half, 8), half), :],
            send_sem=g_send.at[d, c],
            recv_sem=g_recv.at[owner, c],
            device_id=(t_me, peer),
            device_id_type=MESH,
        )

    def own_copy(c):
        part = pl.ds(per * c, per)
        return pltpu.make_async_copy(
            cz.at[part],
            coarse.at[part, pl.ds(pl.multiple_of(w_me * half, 8), half), :],
            own_sem.at[c],
        )

    def finish(c):
        @pl.when(w_has[0])
        def _():
            c_copy(c).wait_recv()

        @pl.loop(per * c, per * c + per)
        def _(i):
            rim = ycr[pl.ds(i, 1), :]
            for h in range(low // 128):
                yb[i, h, TOP - 1 : TOP, :] = rim[:, 128 * h : 128 * h + 128]
                before = yb[i, h, pl.ds(TOP - 1, half, 2), :]
                middle = yb[i, h, pl.ds(TOP, half, 2), :]
                after = yb[i, h, pl.ds(TOP + 1, half, 2), :]
                cz[i, :, 128 * h : 128 * h + 128] = 0.25 * (before + after) + 0.5 * middle

        own_copy(c).start()
        for d in range(1, n_width):
            g_copy(c, w_me, lax.rem(w_me + d, n_width), d).start()

    got_x(PASSES)
    got_y(PASSES, EDGE)
    residual_plane(planes, planes, 0)
    q[planes] = restrict_height(1)[0]

    @pl.when(t_has[1])
    def _():
        q_copy().start()

    for c in order:
        got_y(PASSES, c)
        if c == 0:
            residual_plane(1, planes + 1, 1)

        @pl.loop(max(span * c, 2), span * c + span)
        def _(p):
            residual_plane(p, p, p - span * c)

        skip = 1 if c == 0 else 0
        q[span * c + skip : span * c + span] = restrict_height(span)[skip:]
        if c == 0:

            @pl.when(t_has[0])
            def _():
                q_copy().wait_recv()

        @pl.loop(per * c, per * c + per)
        def _(i):
            y = 0.25 * (q[2 * i] + q[2 * i + 2]) + 0.5 * q[2 * i + 1]
            for h in range(low // 128):
                yb[i, h, pl.ds(TOP, rows), :] = y[:, 128 * h : 128 * h + 128]
            ycs[pl.ds(i, 1), :] = y[rows - 1 : rows, :]

        @pl.when(w_has[1])
        def _():
            c_copy(c).start()

        if c < CHUNKS - 1:
            finish(c + 1)
    finish(0)

    for k in (PASSES - 1, PASSES):
        sent_x(k)
    for k in range(PASSES + 1):
        for c in (EDGE,) if k == 0 else range(CHUNKS + 1):
            sent_y(k, c)

    @pl.when(t_has[1])
    def _():
        q_copy().wait_send()

    for c in range(CHUNKS):
        stores[c].wait()
        own_copy(c).wait()

        @pl.when(w_has[1])
        def _():
            c_copy(c).wait_send()

        for d in range(1, n_width):
            peer = lax.rem(w_me + d, n_width)
            g_copy(c, w_me, peer, d).wait_send()
            g_copy(c, peer, peer, d).wait_recv()


def solution(mesh):
    n_tunnel, n_width = mesh.shape["tunnel"], mesh.shape["width"]

    def per_device(source, initial, diffusivity, reaction):
        planes, rows, height = source.shape
        low, half = height // 2, rows // 2
        f32 = jnp.float32
        field = (planes, rows, height)
        padded = (planes + 2, rows + 2 * TOP, height)
        columns = (PASSES + 1, 2, planes + 8, height)
        dma = pltpu.SemaphoreType.DMA
        return pl.pallas_call(
            functools.partial(kernel, n_tunnel, n_width),
            out_shape=(
                jax.ShapeDtypeStruct(field, f32),
                jax.ShapeDtypeStruct((planes // 2, half * n_width, low), f32),
            ),
            in_specs=[pl.BlockSpec(memory_space=pl.ANY)] * 4,
            out_specs=(pl.BlockSpec(memory_space=pl.ANY),) * 2,
            scratch_shapes=[
                pltpu.VMEM(padded, f32),
                pltpu.VMEM(padded, f32),
                pltpu.VMEM(field, f32),
                pltpu.VMEM(field, f32),
                pltpu.VMEM(field, f32),
                pltpu.VMEM(field, f32),
                pltpu.VMEM(columns, f32),
                pltpu.VMEM(columns, f32),
                pltpu.VMEM((planes // CHUNKS, rows, height), f32),
                pltpu.VMEM((height, low), jnp.bfloat16),
                pltpu.VMEM((planes + 1, rows, low), f32),
                pltpu.VMEM((planes // 2, low // 128, rows + TOP, 128), f32),
                pltpu.VMEM((planes // 2, low), f32),
                pltpu.VMEM((planes // 2, low), f32),
                pltpu.VMEM((planes // 2, half, low), f32),
                dma((PASSES + 1, 2)),
                dma((PASSES + 1, 2)),
                dma((PASSES + 1, 2, CHUNKS + 1)),
                dma((PASSES + 1, 2, CHUNKS + 1)),
                dma((2,)),
                dma((CHUNKS,)),
                dma((CHUNKS,)),
                dma((n_width, CHUNKS)),
                dma((n_width, CHUNKS)),
                dma((3, CHUNKS)),
                dma(()),
                dma((CHUNKS,)),
                dma((CHUNKS,)),
            ],
            compiler_params=pltpu.CompilerParams(
                collective_id=0, has_side_effects=True, vmem_limit_bytes=58 * 2**20
            ),
        )(source, initial, diffusivity, reaction)

    return jax.shard_map(
        per_device,
        mesh=mesh,
        in_specs=(P("tunnel", "width", None),) * 4,
        out_specs=(P("tunnel", "width", None), P("tunnel", None, None)),
        check_vma=False,
    )
```

```python
import functools

import jax
import jax.numpy as jnp
from jax import lax
from jax.experimental import pallas as pl
from jax.experimental.pallas import tpu as pltpu
from jax.sharding import PartitionSpec as P

PASSES = 4
CHUNKS = 4
EDGE = CHUNKS
TOP = 8

relax_weight = 0.8
settle_rate = 0.5
MESH = pl.DeviceIdType.MESH


def kernel(
    n_tunnel,
    n_width,
    source,
    initial,
    diffusivity,
    reaction,
    smoothed,
    coarse,
    va,
    vb,
    src,
    dif,
    rea,
    rec,
    ys,
    yr,
    resid,
    table,
    q,
    yb,
    ycs,
    ycr,
    cz,
    x_send,
    x_recv,
    y_send,
    y_recv,
    q_sem,
    c_send,
    c_recv,
    g_send,
    g_recv,
    in_sem,
    v_sem,
    out_sem,
    own_sem,
):
    planes, rows, height = source.shape
    span = planes // CHUNKS
    tiles = rows // 8
    half = rows // 2
    low = height // 2
    per = span // 2
    t_me = lax.axis_index("tunnel")
    w_me = lax.axis_index("width")
    t_has = (t_me > 0, t_me < n_tunnel - 1)
    w_has = (w_me > 0, w_me < n_width - 1)
    t_to = (
        (jnp.maximum(t_me - 1, 0), w_me),
        (jnp.minimum(t_me + 1, n_tunnel - 1), w_me),
    )
    w_to = (
        (t_me, jnp.maximum(w_me - 1, 0)),
        (t_me, jnp.minimum(w_me + 1, n_width - 1)),
    )
    bufs = (va, vb)
    cells = pl.ds(TOP, rows)

    def bounds(c):
        first = max(span * c - 1, 0)
        last = planes if c == CHUNKS - 1 else span * c + span - 1
        return first, last - first

    load_v = pltpu.make_async_copy(initial, va.at[pl.ds(1, planes), cells, :], v_sem)
    load_v.start()
    loads = {}
    for c in (CHUNKS - 1, 0) + tuple(range(CHUNKS - 2, 0, -1)):
        first, count = bounds(c)
        for a, (hbm, mem) in enumerate(((source, src), (diffusivity, dif), (reaction, rea))):
            loads[a, c] = pltpu.make_async_copy(
                hbm.at[pl.ds(first, count)], mem.at[pl.ds(first, count)], in_sem.at[a, c]
            )
            loads[a, c].start()

    barrier = pltpu.get_barrier_semaphore()
    for d in range(2):

        @pl.when(t_has[d])
        def _():
            pl.semaphore_signal(barrier, inc=1, device_id=t_to[d], device_id_type=MESH)

        @pl.when(w_has[d])
        def _():
            pl.semaphore_signal(barrier, inc=1, device_id=w_to[d], device_id_type=MESH)

    for d in range(2):

        @pl.when(jnp.logical_not(t_has[d]))
        def _():
            side = 0 if d == 0 else planes + 1
            for buf in bufs:
                buf[side, cells, :] = jnp.zeros((rows, height), jnp.float32)
            if d == 0:
                q[0] = jnp.zeros((rows, low), jnp.float32)

        @pl.when(jnp.logical_not(w_has[d]))
        def _():
            for k in range(PASSES + 1):
                yr[k, d] = jnp.zeros(yr.shape[2:], jnp.float32)
            if d == 0:
                ycr[...] = jnp.zeros(ycr.shape, jnp.float32)

    fine = lax.broadcasted_iota(jnp.int32, (height, low), 0)
    gap = fine - 2 * lax.broadcasted_iota(jnp.int32, (height, low), 1)
    weight = jnp.where(gap == 0, 0.5, jnp.where((gap == 1) | (gap == -1), 0.25, 0.0))
    table[...] = weight.astype(jnp.float32).astype(jnp.bfloat16)

    beside = sum(jnp.where(has, 1, 0) for has in t_has + w_has)
    pl.semaphore_wait(barrier, beside)

    def x_copy(k, d):
        buf = bufs[k % 2]
        mine, theirs = (1, planes + 1) if d == 0 else (planes, 0)
        return pltpu.make_async_remote_copy(
            src_ref=buf.at[mine, cells, :],
            dst_ref=buf.at[theirs, cells, :],
            send_sem=x_send.at[k, d],
            recv_sem=x_recv.at[k, 1 - d],
            device_id=t_to[d],
            device_id_type=MESH,
        )

    def y_copy(k, d, c):
        if k == 0:
            part = pl.ds(0, ys.shape[2])
        elif c == EDGE:
            part = pl.ds(planes, 8)
        else:
            part = pl.ds(span * c, span)
        return pltpu.make_async_remote_copy(
            src_ref=ys.at[k, d, part, :],
            dst_ref=yr.at[k, 1 - d, part, :],
            send_sem=y_send.at[k, d, c],
            recv_sem=y_recv.at[k, 1 - d, c],
            device_id=w_to[d],
            device_id_type=MESH,
        )

    def start_x(k):
        for d in range(2):

            @pl.when(t_has[d])
            def _():
                x_copy(k, d).start()

    def sent_x(k):
        for d in range(2):

            @pl.when(t_has[d])
            def _():
                x_copy(k, d).wait_send()

    def got_x(k):
        for d in range(2):

            @pl.when(t_has[d])
            def _():
                x_copy(k, 1 - d).wait_recv()

    def start_y(k, c):
        for d in range(2):

            @pl.when(w_has[d])
            def _():
                y_copy(k, d, c).start()

    def sent_y(k, c):
        for d in range(2):

            @pl.when(w_has[d])
            def _():
                y_copy(k, d, c).wait_send()

    def got_y(k, c):
        for d in range(2):

            @pl.when(w_has[d])
            def _():
                y_copy(k, 1 - d, c).wait_recv()

    lane = lax.broadcasted_iota(jnp.int32, (8, 128), 1)

    def neighbours(v, p, t):
        here = pl.ds(TOP + 8 * t, 8)
        centre = v[p, here, :]
        beside = (
            v[p - 1, here, :]
            + v[p + 1, here, :]
            + (v[p, pl.ds(TOP + 8 * t - 1, 8), :] + v[p, pl.ds(TOP + 8 * t + 1, 8), :])
        )
        parts = [centre[:, z : z + 128] for z in range(0, height, 128)]
        down = [pltpu.roll(part, 127, 1) for part in parts] + [0.0]
        up = [0.0] + [pltpu.roll(part, 1, 1) for part in parts]
        count = len(parts)
        upper = jnp.concatenate(
            [jnp.where(lane == 127, down[j + 1], down[j]) for j in range(count)], axis=1
        )
        lower = jnp.concatenate(
            [jnp.where(lane == 0, up[j], up[j + 1]) for j in range(count)], axis=1
        )
        return centre, 2.5 * beside + 0.5 * (upper + lower), upper

    def put_halo(k, p, row):
        v = bufs[k % 2]
        v[p, TOP - 1 : TOP, :] = yr[k, 0, pl.ds(row, 1), :]
        v[p, TOP + rows : TOP + rows + 1, :] = yr[k, 1, pl.ds(row, 1), :]

    def smooth_plane(k, p, row):
        v, new = bufs[(k - 1) % 2], bufs[k % 2]
        put_halo(k - 1, p, row)
        for t in range(tiles):
            at = pl.ds(8 * t, 8)
            centre, beside, upper = neighbours(v, p, t)
            spread = dif[p - 1, at, :]
            if k == 1:
                factor = relax_weight / (rea[p - 1, at, :] + 11.0 * spread + settle_rate)
                rec[p - 1, at, :] = factor
            else:
                factor = rec[p - 1, at, :]
            off = src[p - 1, at, :] + spread * beside + settle_rate * upper
            out = (1.0 - relax_weight) * centre + factor * off
            new[p, pl.ds(TOP + 8 * t, 8), :] = out
            if t == 0:
                ys[k, 0, pl.ds(row, 1), :] = out[0:1, :]
            if t == tiles - 1:
                ys[k, 1, pl.ds(row, 1), :] = out[7:8, :]

    def residual_plane(p, row, slot):
        v = bufs[PASSES % 2]
        put_halo(PASSES, p, row)
        for t in range(tiles):
            at = pl.ds(8 * t, 8)
            centre, beside, upper = neighbours(v, p, t)
            spread = dif[p - 1, at, :]
            diagonal = rea[p - 1, at, :] + 11.0 * spread + settle_rate
            resid[slot, at, :] = (
                src[p - 1, at, :]
                - diagonal * centre
                + spread * beside
                + settle_rate * upper
            )

    def restrict_height(count):
        r = resid[0:count].reshape(count * rows, height)
        hi = r.astype(jnp.bfloat16)
        lo = (r - hi.astype(jnp.float32)).astype(jnp.bfloat16)
        t = table[...]
        out = jnp.dot(hi, t, preferred_element_type=jnp.float32) + jnp.dot(
            lo, t, preferred_element_type=jnp.float32
        )
        return out.reshape(count, rows, low)

    load_v.wait()
    start_x(0)

    @pl.loop(1, planes + 1)
    def _(p):
        ys[0, 0, pl.ds(p, 1), :] = va[p, TOP : TOP + 1, :]
        ys[0, 1, pl.ds(p, 1), :] = va[p, TOP + rows - 1 : TOP + rows, :]

    ys[0, 0, planes + 1 : planes + 2, :] = va[1, TOP : TOP + 1, :]
    ys[0, 1, planes + 1 : planes + 2, :] = va[1, TOP + rows - 1 : TOP + rows, :]
    start_y(0, EDGE)

    order = tuple(range(CHUNKS - 1, -1, -1))
    stores = {}
    for k in range(1, PASSES + 1):
        if k >= 2:
            sent_x(k - 2)
        if k == 1:
            for c in (CHUNKS - 1, 0):
                for a in range(3):
                    loads[a, c].wait()
        got_x(k - 1)
        got_y(k - 1, EDGE)
        smooth_plane(k, planes, planes)
        smooth_plane(k, 1, planes + 1)
        start_x(k)
        start_y(k, EDGE)
        for c in order:
            if k == 1:
                if 0 < c < CHUNKS - 1:
                    for a in range(3):
                        loads[a, c].wait()
            else:
                got_y(k - 1, c)

            @pl.loop(max(span * c, 2), span * c + span)
            def _(p):
                smooth_plane(k, p, p)

            start_y(k, c)
            if k == PASSES:
                first, count = bounds(c)
                stores[c] = pltpu.make_async_copy(
                    bufs[k % 2].at[pl.ds(first + 1, count), cells, :],
                    smoothed.at[pl.ds(first, count)],
                    out_sem.at[c],
                )
                stores[c].start()

    def q_copy():
        return pltpu.make_async_remote_copy(
            src_ref=q.at[planes],
            dst_ref=q.at[0],
            send_sem=q_sem.at[0],
            recv_sem=q_sem.at[1],
            device_id=t_to[1],
            device_id_type=MESH,
        )

    def c_copy(c):
        part = pl.ds(per * c, per)
        return pltpu.make_async_remote_copy(
            src_ref=ycs.at[part, :],
            dst_ref=ycr.at[part, :],
            send_sem=c_send.at[c],
            recv_sem=c_recv.at[c],
            device_id=w_to[1],
            device_id_type=MESH,
        )

    def g_copy(c, owner, d, mine):
        part = pl.ds(per * c, per)
        place = coarse.at[part, pl.ds(pl.multiple_of(owner * half, 8), half), :]
        return pltpu.make_async_remote_copy(
            src_ref=cz.at[part] if mine else place,
            dst_ref=place,
            send_sem=g_send.at[d, owner, c],
            recv_sem=g_recv.at[owner, c],
            device_id=w_to[d],
            device_id_type=MESH,
        )

    def own_copy(c):
        part = pl.ds(per * c, per)
        return pltpu.make_async_copy(
            cz.at[part],
            coarse.at[part, pl.ds(pl.multiple_of(w_me * half, 8), half), :],
            own_sem.at[c],
        )

    def finish(c):
        @pl.when(w_has[0])
        def _():
            c_copy(c).wait_recv()

        @pl.loop(per * c, per * c + per)
        def _(i):
            rim = ycr[pl.ds(i, 1), :]
            for h in range(low // 128):
                yb[i, h, TOP - 1 : TOP, :] = rim[:, 128 * h : 128 * h + 128]
                before = yb[i, h, pl.ds(TOP - 1, half, 2), :]
                middle = yb[i, h, pl.ds(TOP, half, 2), :]
                after = yb[i, h, pl.ds(TOP + 1, half, 2), :]
                cz[i, :, 128 * h : 128 * h + 128] = 0.25 * (before + after) + 0.5 * middle

        own_copy(c).start()
        for d in range(2):

            @pl.when(w_has[d])
            def _():
                g_copy(c, w_me, d, True).start()

    got_x(PASSES)
    got_y(PASSES, EDGE)
    residual_plane(planes, planes, 0)
    q[planes] = restrict_height(1)[0]

    @pl.when(t_has[1])
    def _():
        q_copy().start()

    for c in order:
        got_y(PASSES, c)
        if c == 0:
            residual_plane(1, planes + 1, 1)

        @pl.loop(max(span * c, 2), span * c + span)
        def _(p):
            residual_plane(p, p, p - span * c)

        skip = 1 if c == 0 else 0
        q[span * c + skip : span * c + span] = restrict_height(span)[skip:]
        if c == 0:

            @pl.when(t_has[0])
            def _():
                q_copy().wait_recv()

        @pl.loop(per * c, per * c + per)
        def _(i):
            y = 0.25 * (q[2 * i] + q[2 * i + 2]) + 0.5 * q[2 * i + 1]
            for h in range(low // 128):
                yb[i, h, pl.ds(TOP, rows), :] = y[:, 128 * h : 128 * h + 128]
            ycs[pl.ds(i, 1), :] = y[rows - 1 : rows, :]

        @pl.when(w_has[1])
        def _():
            c_copy(c).start()

        if c < CHUNKS - 1:
            finish(c + 1)
    finish(0)

    for step in range(1, n_width):
        for c in order:
            for d in range(2):
                owner = w_me - step if d == 1 else w_me + step

                @pl.when(owner >= 0 if d == 1 else owner < n_width)
                def _():
                    g_copy(c, owner, d, False).wait_recv()

                    @pl.when(w_has[d])
                    def _():
                        g_copy(c, owner, d, False).start()

    for k in (PASSES - 1, PASSES):
        sent_x(k)
    for k in range(PASSES + 1):
        for c in (EDGE,) if k == 0 else range(CHUNKS + 1):
            sent_y(k, c)

    @pl.when(t_has[1])
    def _():
        q_copy().wait_send()

    for c in range(CHUNKS):
        stores[c].wait()
        own_copy(c).wait()

        @pl.when(w_has[1])
        def _():
            c_copy(c).wait_send()

        for owner in range(n_width):
            for d in range(2):
                goes = owner <= w_me if d == 1 else owner >= w_me

                @pl.when(jnp.logical_and(w_has[d], goes))
                def _():
                    g_copy(c, owner, d, False).wait_send()


def solution(mesh):
    n_tunnel, n_width = mesh.shape["tunnel"], mesh.shape["width"]

    def per_device(source, initial, diffusivity, reaction):
        planes, rows, height = source.shape
        low, half = height // 2, rows // 2
        f32 = jnp.float32
        field = (planes, rows, height)
        padded = (planes + 2, rows + 2 * TOP, height)
        columns = (PASSES + 1, 2, planes + 8, height)
        dma = pltpu.SemaphoreType.DMA
        return pl.pallas_call(
            functools.partial(kernel, n_tunnel, n_width),
            out_shape=(
                jax.ShapeDtypeStruct(field, f32),
                jax.ShapeDtypeStruct((planes // 2, half * n_width, low), f32),
            ),
            in_specs=[pl.BlockSpec(memory_space=pl.ANY)] * 4,
            out_specs=(pl.BlockSpec(memory_space=pl.ANY),) * 2,
            scratch_shapes=[
                pltpu.VMEM(padded, f32),
                pltpu.VMEM(padded, f32),
                pltpu.VMEM(field, f32),
                pltpu.VMEM(field, f32),
                pltpu.VMEM(field, f32),
                pltpu.VMEM(field, f32),
                pltpu.VMEM(columns, f32),
                pltpu.VMEM(columns, f32),
                pltpu.VMEM((planes // CHUNKS, rows, height), f32),
                pltpu.VMEM((height, low), jnp.bfloat16),
                pltpu.VMEM((planes + 1, rows, low), f32),
                pltpu.VMEM((planes // 2, low // 128, rows + TOP, 128), f32),
                pltpu.VMEM((planes // 2, low), f32),
                pltpu.VMEM((planes // 2, low), f32),
                pltpu.VMEM((planes // 2, half, low), f32),
                dma((PASSES + 1, 2)),
                dma((PASSES + 1, 2)),
                dma((PASSES + 1, 2, CHUNKS + 1)),
                dma((PASSES + 1, 2, CHUNKS + 1)),
                dma((2,)),
                dma((CHUNKS,)),
                dma((CHUNKS,)),
                dma((2, n_width, CHUNKS)),
                dma((n_width, CHUNKS)),
                dma((3, CHUNKS)),
                dma(()),
                dma((CHUNKS,)),
                dma((CHUNKS,)),
            ],
            compiler_params=pltpu.CompilerParams(
                collective_id=0, has_side_effects=True, vmem_limit_bytes=58 * 2**20
            ),
        )(source, initial, diffusivity, reaction)

    return jax.shard_map(
        per_device,
        mesh=mesh,
        in_specs=(P("tunnel", "width", None),) * 4,
        out_specs=(P("tunnel", "width", None), P("tunnel", None, None)),
        check_vma=False,
    )
```

```python
import functools

import jax
import jax.numpy as jnp
from jax import lax
from jax.experimental import pallas as pl
from jax.experimental.pallas import tpu as pltpu
from jax.sharding import PartitionSpec as P

PASSES = 4
CHUNKS = 4
EDGE = CHUNKS
TOP = 8

relax_weight = 0.8
settle_rate = 0.5
MESH = pl.DeviceIdType.MESH


def kernel(
    n_tunnel,
    n_width,
    source,
    initial,
    diffusivity,
    reaction,
    smoothed,
    coarse,
    va,
    vb,
    src,
    dif,
    rea,
    rec,
    ys,
    yr,
    resid,
    table,
    q,
    yb,
    ycs,
    ycr,
    cz,
    x_send,
    x_recv,
    y_send,
    y_recv,
    q_sem,
    c_send,
    c_recv,
    g_send,
    g_recv,
    in_sem,
    v_sem,
    out_sem,
    own_sem,
):
    planes, rows, height = source.shape
    span = planes // CHUNKS
    tiles = rows // 8
    half = rows // 2
    low = height // 2
    per = span // 2
    t_me = lax.axis_index("tunnel")
    w_me = lax.axis_index("width")
    t_has = (t_me > 0, t_me < n_tunnel - 1)
    w_has = (w_me > 0, w_me < n_width - 1)
    t_to = (
        (jnp.maximum(t_me - 1, 0), w_me),
        (jnp.minimum(t_me + 1, n_tunnel - 1), w_me),
    )
    w_to = (
        (t_me, jnp.maximum(w_me - 1, 0)),
        (t_me, jnp.minimum(w_me + 1, n_width - 1)),
    )
    bufs = (va, vb)
    cells = pl.ds(TOP, rows)

    def bounds(c):
        first = max(span * c - 1, 0)
        last = planes if c == CHUNKS - 1 else span * c + span - 1
        return first, last - first

    load_v = pltpu.make_async_copy(initial, va.at[pl.ds(1, planes), cells, :], v_sem)
    load_v.start()
    loads = {}
    for c in (CHUNKS - 1, 0) + tuple(range(CHUNKS - 2, 0, -1)):
        first, count = bounds(c)
        for a, (hbm, mem) in enumerate(((source, src), (diffusivity, dif), (reaction, rea))):
            loads[a, c] = pltpu.make_async_copy(
                hbm.at[pl.ds(first, count)], mem.at[pl.ds(first, count)], in_sem.at[a, c]
            )
            loads[a, c].start()

    barrier = pltpu.get_barrier_semaphore()
    for d in range(2):

        @pl.when(t_has[d])
        def _():
            pl.semaphore_signal(barrier, inc=1, device_id=t_to[d], device_id_type=MESH)

        @pl.when(w_has[d])
        def _():
            pl.semaphore_signal(barrier, inc=1, device_id=w_to[d], device_id_type=MESH)

    for d in range(2):

        @pl.when(jnp.logical_not(t_has[d]))
        def _():
            side = 0 if d == 0 else planes + 1
            for buf in bufs:
                buf[side, cells, :] = jnp.zeros((rows, height), jnp.float32)
            if d == 0:
                q[0] = jnp.zeros((rows, low), jnp.float32)

        @pl.when(jnp.logical_not(w_has[d]))
        def _():
            for k in range(PASSES + 1):
                yr[k, d] = jnp.zeros(yr.shape[2:], jnp.float32)
            if d == 0:
                ycr[...] = jnp.zeros(ycr.shape, jnp.float32)

    fine = lax.broadcasted_iota(jnp.int32, (height, low), 0)
    gap = fine - 2 * lax.broadcasted_iota(jnp.int32, (height, low), 1)
    weight = jnp.where(gap == 0, 0.5, jnp.where((gap == 1) | (gap == -1), 0.25, 0.0))
    table[...] = weight.astype(jnp.float32).astype(jnp.bfloat16)

    beside = sum(jnp.where(has, 1, 0) for has in t_has + w_has)
    pl.semaphore_wait(barrier, beside)

    def x_copy(k, d):
        buf = bufs[k % 2]
        mine, theirs = (1, planes + 1) if d == 0 else (planes, 0)
        return pltpu.make_async_remote_copy(
            src_ref=buf.at[mine, cells, :],
            dst_ref=buf.at[theirs, cells, :],
            send_sem=x_send.at[k, d],
            recv_sem=x_recv.at[k, 1 - d],
            device_id=t_to[d],
            device_id_type=MESH,
        )

    def y_copy(k, d, c):
        if k == 0:
            part = pl.ds(0, ys.shape[2])
        elif c == EDGE:
            part = pl.ds(planes, 8)
        else:
            part = pl.ds(span * c, span)
        return pltpu.make_async_remote_copy(
            src_ref=ys.at[k, d, part, :],
            dst_ref=yr.at[k, 1 - d, part, :],
            send_sem=y_send.at[k, d, c],
            recv_sem=y_recv.at[k, 1 - d, c],
            device_id=w_to[d],
            device_id_type=MESH,
        )

    def start_x(k):
        for d in range(2):

            @pl.when(t_has[d])
            def _():
                x_copy(k, d).start()

    def sent_x(k):
        for d in range(2):

            @pl.when(t_has[d])
            def _():
                x_copy(k, d).wait_send()

    def got_x(k):
        for d in range(2):

            @pl.when(t_has[d])
            def _():
                x_copy(k, 1 - d).wait_recv()

    def start_y(k, c):
        for d in range(2):

            @pl.when(w_has[d])
            def _():
                y_copy(k, d, c).start()

    def sent_y(k, c):
        for d in range(2):

            @pl.when(w_has[d])
            def _():
                y_copy(k, d, c).wait_send()

    def got_y(k, c):
        for d in range(2):

            @pl.when(w_has[d])
            def _():
                y_copy(k, 1 - d, c).wait_recv()

    lane = lax.broadcasted_iota(jnp.int32, (8, 128), 1)

    def neighbours(v, p, t):
        here = pl.ds(TOP + 8 * t, 8)
        centre = v[p, here, :]
        beside = (
            v[p - 1, here, :]
            + v[p + 1, here, :]
            + (v[p, pl.ds(TOP + 8 * t - 1, 8), :] + v[p, pl.ds(TOP + 8 * t + 1, 8), :])
        )
        parts = [centre[:, z : z + 128] for z in range(0, height, 128)]
        down = [pltpu.roll(part, 127, 1) for part in parts] + [0.0]
        up = [0.0] + [pltpu.roll(part, 1, 1) for part in parts]
        count = len(parts)
        upper = jnp.concatenate(
            [jnp.where(lane == 127, down[j + 1], down[j]) for j in range(count)], axis=1
        )
        lower = jnp.concatenate(
            [jnp.where(lane == 0, up[j], up[j + 1]) for j in range(count)], axis=1
        )
        return centre, 2.5 * beside + 0.5 * (upper + lower), upper

    def put_halo(k, p, row):
        v = bufs[k % 2]
        v[p, TOP - 1 : TOP, :] = yr[k, 0, pl.ds(row, 1), :]
        v[p, TOP + rows : TOP + rows + 1, :] = yr[k, 1, pl.ds(row, 1), :]

    def put_halos(k, c):
        @pl.loop(max(span * c, 2), span * c + span, unroll=2)
        def _(p):
            put_halo(k, p, p)

    def smooth_plane(k, p, row):
        v, new = bufs[(k - 1) % 2], bufs[k % 2]
        for t in range(tiles):
            at = pl.ds(8 * t, 8)
            centre, beside, upper = neighbours(v, p, t)
            spread = dif[p - 1, at, :]
            if k == 1:
                factor = relax_weight / (rea[p - 1, at, :] + 11.0 * spread + settle_rate)
                rec[p - 1, at, :] = factor
            else:
                factor = rec[p - 1, at, :]
            off = src[p - 1, at, :] + spread * beside + settle_rate * upper
            out = (1.0 - relax_weight) * centre + factor * off
            new[p, pl.ds(TOP + 8 * t, 8), :] = out
            if t == 0:
                ys[k, 0, pl.ds(row, 1), :] = out[0:1, :]
            if t == tiles - 1:
                ys[k, 1, pl.ds(row, 1), :] = out[7:8, :]

    def residual_plane(p, row, slot):
        v = bufs[PASSES % 2]
        for t in range(tiles):
            at = pl.ds(8 * t, 8)
            centre, beside, upper = neighbours(v, p, t)
            spread = dif[p - 1, at, :]
            diagonal = rea[p - 1, at, :] + 11.0 * spread + settle_rate
            resid[slot, at, :] = (
                src[p - 1, at, :]
                - diagonal * centre
                + spread * beside
                + settle_rate * upper
            )

    def restrict_height(count):
        r = resid[0:count].reshape(count * rows, height)
        hi = r.astype(jnp.bfloat16)
        lo = (r - hi.astype(jnp.float32)).astype(jnp.bfloat16)
        t = table[...]
        out = jnp.dot(hi, t, preferred_element_type=jnp.float32) + jnp.dot(
            lo, t, preferred_element_type=jnp.float32
        )
        return out.reshape(count, rows, low)

    order = tuple(range(CHUNKS - 1, -1, -1))

    def q_copy():
        return pltpu.make_async_remote_copy(
            src_ref=q.at[planes],
            dst_ref=q.at[0],
            send_sem=q_sem.at[0],
            recv_sem=q_sem.at[1],
            device_id=t_to[1],
            device_id_type=MESH,
        )

    def c_copy(c):
        return pltpu.make_async_remote_copy(
            src_ref=ycs.at[c],
            dst_ref=ycr.at[c],
            send_sem=c_send.at[c],
            recv_sem=c_recv.at[c],
            device_id=w_to[1],
            device_id_type=MESH,
        )

    def g_copy(c, owner, d, mine):
        part = pl.ds(per * c, per)
        place = coarse.at[part, pl.ds(pl.multiple_of(owner * half, 8), half), :]
        return pltpu.make_async_remote_copy(
            src_ref=cz.at[part] if mine else place,
            dst_ref=place,
            send_sem=g_send.at[d, owner, c],
            recv_sem=g_recv.at[owner, c],
            device_id=w_to[d],
            device_id_type=MESH,
        )

    def own_copy(c):
        part = pl.ds(per * c, per)
        return pltpu.make_async_copy(
            cz.at[part],
            coarse.at[part, pl.ds(pl.multiple_of(w_me * half, 8), half), :],
            own_sem.at[c],
        )

    def finish(c):
        @pl.when(w_has[0])
        def _():
            c_copy(c).wait_recv()

        @pl.loop(per * c, per * c + per)
        def _(i):
            rim = ycr[c, pl.ds(i - per * c, 1), :]
            for h in range(low // 128):
                yb[i, h, TOP - 1 : TOP, :] = rim[:, 128 * h : 128 * h + 128]
                before = yb[i, h, pl.ds(TOP - 1, half, 2), :]
                middle = yb[i, h, pl.ds(TOP, half, 2), :]
                after = yb[i, h, pl.ds(TOP + 1, half, 2), :]
                cz[i, :, 128 * h : 128 * h + 128] = 0.25 * (before + after) + 0.5 * middle

        own_copy(c).start()
        for d in range(2):

            @pl.when(w_has[d])
            def _():
                g_copy(c, w_me, d, True).start()

    def residual_edge():
        got_x(PASSES)
        got_y(PASSES, EDGE)
        put_halo(PASSES, planes, planes)
        residual_plane(planes, planes, 0)
        q[planes] = restrict_height(1)[0]

        @pl.when(t_has[1])
        def _():
            q_copy().start()

    def residual_part(c):
        got_y(PASSES, c)
        if c == 0:
            put_halo(PASSES, 1, planes + 1)
            residual_plane(1, planes + 1, 1)

        put_halos(PASSES, c)

        @pl.loop(max(span * c, 2), span * c + span, unroll=4 if c else 7)
        def _(p):
            residual_plane(p, p, p - span * c)

        skip = 1 if c == 0 else 0
        q[span * c + skip : span * c + span] = restrict_height(span)[skip:]
        if c == 0:

            @pl.when(t_has[0])
            def _():
                q_copy().wait_recv()

        @pl.loop(per * c, per * c + per)
        def _(i):
            y = 0.25 * (q[2 * i] + q[2 * i + 2]) + 0.5 * q[2 * i + 1]
            for h in range(low // 128):
                yb[i, h, pl.ds(TOP, rows), :] = y[:, 128 * h : 128 * h + 128]
            ycs[c, pl.ds(i - per * c, 1), :] = y[rows - 1 : rows, :]

        @pl.when(w_has[1])
        def _():
            c_copy(c).start()

    def forward(turn):
        for step in range(1, n_width):
            c = CHUNKS - 1 - (turn - step)
            if not 0 <= c < CHUNKS:
                continue
            for d in range(2):
                owner = w_me - step if d == 1 else w_me + step

                @pl.when(owner >= 0 if d == 1 else owner < n_width)
                def _():
                    g_copy(c, owner, d, False).wait_recv()

                    @pl.when(w_has[d])
                    def _():
                        g_copy(c, owner, d, False).start()

    def finish_and_forward(c):
        finish(c)
        forward(CHUNKS - 1 - c)

    load_v.wait()
    start_x(0)

    @pl.loop(1, planes + 1)
    def _(p):
        ys[0, 0, pl.ds(p, 1), :] = va[p, TOP : TOP + 1, :]
        ys[0, 1, pl.ds(p, 1), :] = va[p, TOP + rows - 1 : TOP + rows, :]

    ys[0, 0, planes + 1 : planes + 2, :] = va[1, TOP : TOP + 1, :]
    ys[0, 1, planes + 1 : planes + 2, :] = va[1, TOP + rows - 1 : TOP + rows, :]
    start_y(0, EDGE)

    stores = {}
    for k in range(1, PASSES + 1):
        if k >= 2:
            sent_x(k - 2)
        if k == 1:
            for c in (CHUNKS - 1, 0):
                for a in range(3):
                    loads[a, c].wait()
        got_x(k - 1)
        got_y(k - 1, EDGE)
        put_halo(k - 1, planes, planes)
        put_halo(k - 1, 1, planes + 1)
        smooth_plane(k, planes, planes)
        smooth_plane(k, 1, planes + 1)
        start_x(k)
        start_y(k, EDGE)
        for c in order:
            if k == 1:
                if 0 < c < CHUNKS - 1:
                    for a in range(3):
                        loads[a, c].wait()
            else:
                got_y(k - 1, c)

            put_halos(k - 1, c)

            @pl.loop(max(span * c, 2), span * c + span, unroll=4 if c else 7)
            def _(p):
                smooth_plane(k, p, p)

            start_y(k, c)
            if k == PASSES:
                first, count = bounds(c)
                stores[c] = pltpu.make_async_copy(
                    bufs[k % 2].at[pl.ds(first + 1, count), cells, :],
                    smoothed.at[pl.ds(first, count)],
                    out_sem.at[c],
                )
                stores[c].start()
                if c < CHUNKS - 2:
                    finish_and_forward(c + 2)
                if c == CHUNKS - 2:
                    residual_edge()
                if c < CHUNKS - 1:
                    residual_part(c + 1)

    residual_part(0)
    finish_and_forward(1)
    finish_and_forward(0)
    for turn in range(CHUNKS, CHUNKS + n_width - 1):
        forward(turn)


    for k in (PASSES - 1, PASSES):
        sent_x(k)
    for k in range(PASSES + 1):
        for c in (EDGE,) if k == 0 else range(CHUNKS + 1):
            sent_y(k, c)

    @pl.when(t_has[1])
    def _():
        q_copy().wait_send()

    for c in range(CHUNKS):
        stores[c].wait()
        own_copy(c).wait()

        @pl.when(w_has[1])
        def _():
            c_copy(c).wait_send()

        for owner in range(n_width):
            for d in range(2):
                goes = owner <= w_me if d == 1 else owner >= w_me

                @pl.when(jnp.logical_and(w_has[d], goes))
                def _():
                    g_copy(c, owner, d, False).wait_send()


def solution(mesh):
    n_tunnel, n_width = mesh.shape["tunnel"], mesh.shape["width"]

    def per_device(source, initial, diffusivity, reaction):
        planes, rows, height = source.shape
        low, half = height // 2, rows // 2
        f32 = jnp.float32
        field = (planes, rows, height)
        padded = (planes + 2, rows + 2 * TOP, height)
        columns = (PASSES + 1, 2, planes + 8, height)
        dma = pltpu.SemaphoreType.DMA
        return pl.pallas_call(
            functools.partial(kernel, n_tunnel, n_width),
            out_shape=(
                jax.ShapeDtypeStruct(field, f32),
                jax.ShapeDtypeStruct((planes // 2, half * n_width, low), f32),
            ),
            in_specs=[pl.BlockSpec(memory_space=pl.ANY)] * 4,
            out_specs=(pl.BlockSpec(memory_space=pl.ANY),) * 2,
            scratch_shapes=[
                pltpu.VMEM(padded, f32),
                pltpu.VMEM(padded, f32),
                pltpu.VMEM(field, f32),
                pltpu.VMEM(field, f32),
                pltpu.VMEM(field, f32),
                pltpu.VMEM(field, f32),
                pltpu.VMEM(columns, f32),
                pltpu.VMEM(columns, f32),
                pltpu.VMEM((planes // CHUNKS, rows, height), f32),
                pltpu.VMEM((height, low), jnp.bfloat16),
                pltpu.VMEM((planes + 1, rows, low), f32),
                pltpu.VMEM((planes // 2, low // 128, rows + TOP, 128), f32),
                pltpu.VMEM((CHUNKS, 8, low), f32),
                pltpu.VMEM((CHUNKS, 8, low), f32),
                pltpu.VMEM((planes // 2, half, low), f32),
                dma((PASSES + 1, 2)),
                dma((PASSES + 1, 2)),
                dma((PASSES + 1, 2, CHUNKS + 1)),
                dma((PASSES + 1, 2, CHUNKS + 1)),
                dma((2,)),
                dma((CHUNKS,)),
                dma((CHUNKS,)),
                dma((2, n_width, CHUNKS)),
                dma((n_width, CHUNKS)),
                dma((3, CHUNKS)),
                dma(()),
                dma((CHUNKS,)),
                dma((CHUNKS,)),
            ],
            compiler_params=pltpu.CompilerParams(
                collective_id=0, has_side_effects=True, vmem_limit_bytes=58 * 2**20
            ),
        )(source, initial, diffusivity, reaction)

    return jax.shard_map(
        per_device,
        mesh=mesh,
        in_specs=(P("tunnel", "width", None),) * 4,
        out_specs=(P("tunnel", "width", None), P("tunnel", None, None)),
        check_vma=False,
    )
```
